32 devices in a mesh: rep: 4 (over y, x), exp: 8 (over z, core).
Axes of the slice: x: 2, y: 2, z: 4, core: 2. Of those that a mesh axis runs over, the one named last changes fastest.
Arguments:
- tokens: bfloat16 [4096, 2048], P(('rep', 'exp')), may hold values from -6 to 6
- grad_out: bfloat16 [4096, 2048], P(('rep', 'exp')), may hold values from -6 to 6
- routes: int32 [4096, 2], P(('rep', 'exp')), may hold values from 0 to 7, all different within a row; in each aligned block of 128 rows (0 to 127, 128 to 255, ...) at most 64 rows name the same one
- gates: float32 [4096, 2], P(('rep', 'exp')), may hold values from 0.1 to 1
- w_gate: bfloat16 [8, 2048, 768], P('exp', 'rep'), may hold values from -0.125 to 0.125
- w_up: bfloat16 [8, 2048, 768], P('exp', 'rep'), may hold values from -0.125 to 0.125
- w_down: bfloat16 [8, 2048, 768], P('exp', 'rep'), may hold values from -0.125 to 0.125
Outputs:
- grad_gate: float32 [8, 2048, 768], P('exp', 'rep')
- grad_up: float32 [8, 2048, 768], P('exp', 'rep')
- grad_down: float32 [8, 2048, 768], P('exp', 'rep')
- grad_in: bfloat16 [4096, 2048], P(('rep', 'exp'))
The draws below stay inside these ranges and needn't reach their ends.
Inputs may be any that keep to these rules, and one draw needn't show every extreme that they name: `routes`: each row names 2 different experts. Among the 128 rows of one device no expert is named more than 64 times, and in every draw some device names some expert exactly 64 times; every expert is named somewhere.
All inputs are finite; a program needn't handle non-finite values.
Results may differ from the reference program's by a relative error of at most 0.0065.
Values may be sent and summed in bfloat16 or wider, within the bound.
A program may use at most 128 MiB of HBM per device.

```python
import math
import jax
import jax.numpy as jnp
import numpy as np
from jax import lax

D = 2048
FF = 768
TOPK = 2
TOK_DEV = 128
EXPERTS = 8
CAP = 64
TOKENS = 4096


def levels(key, shape, split, least, largest):
    gain = 1.0
    for dim, parts in split:
        heights = jax.random.uniform(jax.random.fold_in(jax.random.fold_in(key, 6), dim), (parts,), jnp.float32, least / len(split), largest / len(split))
        gain = gain * jnp.repeat(jnp.exp(heights), shape[dim] // parts).reshape((-1,) + (1,) * (len(shape) - 1 - dim))
    return gain


def routed_block(own_key, own, number, rows, number_of, top, reach, skew):
    sequence = jax.random.permutation(own_key, number_of)
    packed, ordinary = load_shares(number_of, rows * top, reach, skew, True), load_shares(number_of, rows * top, reach, skew, False)
    places = jnp.arange(number_of)

    def named(lengths, rotation):
        used = int((lengths > 0).sum())
        fixed = max(1, used // 4)
        passed = fixed + (places - fixed + rotation * (used - fixed)) % max(1, number_of - fixed)
        return jnp.zeros((number_of,), jnp.int32).at[sequence[jnp.where(places < fixed, places, passed)]].set(jnp.asarray(lengths, jnp.int32))

    lengths = jnp.where(number % 4 == 0, named(packed, number // 4), named(ordinary, number - number // 4 - 1))
    mixed = jax.random.permutation(jax.random.fold_in(own, 3), number_of)
    donor, taker = mixed[0:number_of // 2 * 2:2], mixed[1:number_of // 2 * 2:2]
    room = jnp.minimum(lengths[donor] - 1, reach - lengths[taker]) // 2
    room = jnp.where((donor == sequence[0]) | (taker == sequence[0]) | (lengths[taker] == 0), 0, jnp.maximum(room, 0))
    passed = jax.random.randint(jax.random.fold_in(own, 4), (number_of // 2,), 0, 1 << 20) % (room + 1)
    lengths = lengths.at[donor].add(-passed).at[taker].add(passed)
    labels = jnp.searchsorted(jnp.cumsum(lengths), jnp.arange(rows * top), side="right").astype(jnp.int32)
    table = labels.reshape(top, rows).T
    table = table[jax.random.permutation(jax.random.fold_in(own, 1), rows)]
    rotation = jax.random.randint(jax.random.fold_in(own, 2), (rows, 1), 0, top)
    return jnp.take_along_axis(table, (jnp.arange(top)[None, :] + rotation) % top, axis=1)


def load_shares(count, total, most, lean, full):
    portions = [(1 << 20) // math.isqrt(standing ** lean) + 1 for standing in range(1, count + 1)]
    largest = most if full else min(most, max(-(-total // count), total * portions[0] // sum(portions)))
    least = 1 if total - largest >= count - 1 else 0
    given, rest = [largest] + [least] * (count - 1), total - largest - least * (count - 1)
    while rest > 0:
        free = [i for i in range(1, count) if given[i] < largest] or [i for i in range(1, count) if given[i] < most]
        mass, remaining = sum([portions[i] for i in free]), rest
        for i in free:
            extra = min(most - given[i], max(1, remaining * portions[i] // mass), rest)
            given[i] = given[i] + extra
            rest = rest - extra
    return np.array(given)


def scatter_about(key, dims, spread, bound, split=(), held_as=jnp.bfloat16):
    drawn = spread * jax.random.normal(key, dims, jnp.float32)
    if split:
        drawn = drawn * levels(key, dims, split, -0.22, 0.18)
    return jnp.clip(drawn, -bound, bound).astype(held_as)


def setup_inputs(seed: int = 0) -> dict:
    keys = jax.random.split(jax.random.key(seed), 8)
    tokens = scatter_about(keys[0], (TOKENS, D), 1.0, 6.0, ((0, 32),))
    grad_out = scatter_about(keys[1], (TOKENS, D), 1.0, 6.0, ((0, 32),))
    routes_keys = jax.random.split(jax.random.fold_in(keys[2], 1), TOKENS // TOK_DEV)
    routes_turns = jax.random.permutation(jax.random.fold_in(keys[2], 3), TOKENS // TOK_DEV)
    routes = jax.vmap(lambda own, number: routed_block(jax.random.fold_in(keys[2], 2), own, number, TOK_DEV, EXPERTS, TOPK, CAP, 2))(routes_keys, routes_turns).reshape((TOKENS, TOPK))
    gates = jnp.clip(0.1 + 0.9 * jax.random.uniform(keys[3], (TOKENS, TOPK), jnp.float32) ** levels(keys[3], (TOKENS, TOPK), ((0, 32),), -0.2, 0.2), 0.1, 1.0)
    w_gate = scatter_about(keys[4], (EXPERTS, D, FF), D ** -0.5, 0.125, ((0, 8), (1, 4)))
    w_up = scatter_about(keys[5], (EXPERTS, D, FF), D ** -0.5, 0.125, ((0, 8), (1, 4)))
    w_down = scatter_about(keys[6], (EXPERTS, D, FF), D ** -0.5, 0.125, ((0, 8), (1, 4)))
    return {"tokens": tokens, "grad_out": grad_out, "routes": routes, "gates": gates, "w_gate": w_gate, "w_up": w_up, "w_down": w_down}


block_rows = 512


def contract_rows(left, right):
    return lax.dot_general(left, right, (((0,), (0,)), ((), ())), preferred_element_type=jnp.float32)


def against_cols(left, right):
    return lax.dot_general(left, right, (((1,), (1,)), ((), ())), preferred_element_type=jnp.float32)


def reference(tokens, grad_out, routes, gates, w_gate, w_up, w_down):
    tok_total = tokens.shape[0]
    route_total = tok_total * TOPK
    flat_routes = routes.reshape(-1).astype(jnp.int32)
    order = jnp.argsort(flat_routes, stable=True).astype(jnp.int32)
    expert_ids = jnp.arange(EXPERTS, dtype=jnp.int32)
    counts = jnp.sum((flat_routes[:, None] == expert_ids[None, :]).astype(jnp.int32), axis=0)
    starts = (jnp.cumsum(counts) - counts).astype(jnp.int32)
    order_pad = jnp.concatenate([order, jnp.zeros((block_rows,), jnp.int32)])
    scaled_all = (gates[:, :, None].astype(jnp.float32) * grad_out[:, None, :].astype(jnp.float32)).astype(jnp.bfloat16)
    scaled_all = scaled_all.reshape(route_total, D)
    lanes = jnp.arange(block_rows, dtype=jnp.int32)

    def expert_step(accum, expert):
        gate_mat = w_gate[expert]
        up_mat = w_up[expert]
        down_mat = w_down[expert]
        block_count = (counts[expert] + block_rows - 1) // block_rows

        def block_step(block_idx, state):
            dx_acc, acc_gate, acc_up, acc_down = state
            offset = (starts[expert] + block_idx * block_rows).astype(jnp.int32)
            picked = lax.dynamic_slice(order_pad, (offset,), (block_rows,))
            live_mask = (block_idx * block_rows + lanes) < counts[expert]
            tok_ids = picked // TOPK
            x_rows = jnp.where(live_mask[:, None], tokens[tok_ids], jnp.zeros((), jnp.bfloat16))
            g_rows = jnp.where(live_mask[:, None], scaled_all[picked], jnp.zeros((), jnp.bfloat16))
            pre_gate = jnp.dot(x_rows, gate_mat, preferred_element_type=jnp.float32)
            pre_up = jnp.dot(x_rows, up_mat, preferred_element_type=jnp.float32)
            sig_gate = jax.nn.sigmoid(pre_gate)
            silu_gate = pre_gate * sig_gate
            hidden = (silu_gate * pre_up).astype(jnp.bfloat16)
            hid_grad = jnp.dot(g_rows, down_mat, preferred_element_type=jnp.float32)
            d_gate = (hid_grad * pre_up * sig_gate * (1.0 + pre_gate * (1.0 - sig_gate))).astype(jnp.bfloat16)
            d_up = (hid_grad * silu_gate).astype(jnp.bfloat16)
            acc_gate = acc_gate + contract_rows(x_rows, d_gate)
            acc_up = acc_up + contract_rows(x_rows, d_up)
            acc_down = acc_down + contract_rows(g_rows, hidden)
            row_grad = (against_cols(d_gate, gate_mat) + against_cols(d_up, up_mat)).astype(jnp.bfloat16)
            contrib = jnp.where(live_mask[:, None], row_grad.astype(jnp.float32), jnp.zeros((), jnp.float32))
            dx_acc = dx_acc.at[tok_ids].add(contrib)
            return dx_acc, acc_gate, acc_up, acc_down

        zero_grad = jnp.zeros((D, FF), jnp.float32)
        result = lax.fori_loop(0, block_count, block_step, (accum, zero_grad, zero_grad, zero_grad))
        return result[0], (result[1], result[2], result[3])

    dx_total, grads = lax.scan(expert_step, jnp.zeros((tok_total, D), jnp.float32), expert_ids)
    return grads[0], grads[1], grads[2], dx_total.astype(jnp.bfloat16)
```

```python
import functools

import jax
import jax.numpy as jnp
from jax import lax
from jax.experimental import pallas as pl
from jax.experimental.pallas import tpu as pltpu
from jax.sharding import PartitionSpec as P

MESH = pl.DeviceIdType.MESH
F32 = jnp.float32
BF16 = jnp.bfloat16


def contract_rows(left, right):
    return lax.dot_general(left, right, (((0,), (0,)), ((), ())), preferred_element_type=F32)


def against_cols(left, right):
    return lax.dot_general(left, right, (((1,), (1,)), ((), ())), preferred_element_type=F32)


def remote(src, dst, send_sem, recv_sem, rep, exp):
    return pltpu.make_async_remote_copy(
        src_ref=src,
        dst_ref=dst,
        send_sem=send_sem,
        recv_sem=recv_sem,
        device_id=(rep, exp),
        device_id_type=MESH,
    )


def greet(rep, exp, x_rep, y_rep, exp_count):
    barrier = pltpu.get_barrier_semaphore()
    for step in range(1, exp_count):
        other = lax.rem(exp + step, exp_count)
        pl.semaphore_signal(barrier, inc=1, device_id=(rep, other), device_id_type=MESH)
    for other in (x_rep, y_rep):
        pl.semaphore_signal(barrier, inc=1, device_id=(other, exp), device_id_type=MESH)
    pl.semaphore_wait(barrier, exp_count + 1)


def rep_neighbours(rep):
    return rep + 1 - 2 * lax.rem(rep, 2), lax.rem(rep + 2, 4), 3 - rep


def gather_kernel(
    tok, grd, info, wg, wu, wd,
    tok_o, grd_o, info_o, wg_o, wu_o, wd_o,
    row_send, row_recv, info_send, info_recv, w_send, w_fwd, w_recv, local_sem,
):
    rep, exp = lax.axis_index("rep"), lax.axis_index("exp")
    x_rep, y_rep, diag = rep_neighbours(rep)
    z, core = lax.div(exp, 2), lax.rem(exp, 2)
    sibling = exp + 1 - 2 * core
    greet(rep, exp, x_rep, y_rep, 8)

    rows_in, rows_out = (tok, grd), (tok_o, grd_o)
    w_in, w_out = (wg, wu, wd), (wg_o, wu_o, wd_o)
    half = wg.shape[0] // 2
    part = (pl.ds(0, half), pl.ds(half, half))
    targets = (exp + 2, exp - 2, sibling)

    def row_copy(a, block, way, own):
        dst = rows_out[a].at[block]
        return remote(
            rows_in[a] if own else dst, dst,
            row_send.at[a, lax.div(block, 2), way], row_recv.at[a, block], rep, targets[way],
        )

    def row_ways(block, own, up, down, act):
        for a in range(2):
            if up:
                pl.when(z < 3)(lambda a=a: act(row_copy(a, block, 0, own)))
            if down:
                pl.when(z > 0)(lambda a=a: act(row_copy(a, block, 1, own)))
            act(row_copy(a, block, 2, own))

    def start(copy):
        copy.start()

    def sent(copy):
        copy.wait_send()

    def w_own(k, h, way):
        return remote(
            w_in[k].at[part[h]], w_out[k].at[rep, part[h]],
            w_send.at[k, h, way], w_recv.at[k, rep, h], (x_rep, y_rep)[way], exp,
        )

    def w_forward(k, way):
        block, h, to = ((x_rep, 0, y_rep), (y_rep, 1, x_rep))[way]
        ref = w_out[k].at[block, part[h]]
        return remote(ref, ref, w_fwd.at[k, way], w_recv.at[k, block, h], to, exp)

    def w_arrived(k, block, h):
        ref = w_out[k].at[block, part[h]]
        remote(ref, ref, w_fwd.at[k, 0], w_recv.at[k, block, h], y_rep, exp).wait_recv()

    def info_copy(step):
        other = lax.rem(exp + step, 8)
        return remote(
            info, info_o.at[exp], info_send.at[step - 1], info_recv.at[exp], rep, other
        )

    row_ways(exp, True, True, True, start)
    for h in range(2):
        for k in range(3):
            w_own(k, h, 0).start()
            w_own(k, 1 - h, 1).start()
    for step in range(1, 8):
        info_copy(step).start()
    local = [
        pltpu.make_async_copy(tok, tok_o.at[exp], local_sem.at[0]),
        pltpu.make_async_copy(grd, grd_o.at[exp], local_sem.at[1]),
        pltpu.make_async_copy(info, info_o.at[exp], local_sem.at[2]),
        pltpu.make_async_copy(wg, wg_o.at[rep], local_sem.at[3]),
        pltpu.make_async_copy(wu, wu_o.at[rep], local_sem.at[4]),
        pltpu.make_async_copy(wd, wd_o.at[rep], local_sem.at[5]),
    ]
    for copy in local:
        copy.start()

    for s in range(1, 4):
        @pl.when(z >= s)
        def _():
            block = exp - 2 * s
            for a in range(2):
                row_copy(a, block, 2, False).wait_recv()
            row_ways(block, False, True, False, start)

        @pl.when(z + s <= 3)
        def _():
            block = exp + 2 * s
            for a in range(2):
                row_copy(a, block, 2, False).wait_recv()
            row_ways(block, False, False, True, start)

        if s == 1:
            for k in range(3):
                w_arrived(k, x_rep, 0)
                w_forward(k, 0).start()
                w_arrived(k, y_rep, 1)
                w_forward(k, 1).start()

    for k in range(3):
        w_arrived(k, x_rep, 1)
        w_arrived(k, y_rep, 0)
        w_arrived(k, diag, 0)
        w_arrived(k, diag, 1)
    for j in range(4):
        for a in range(2):
            row_copy(a, 2 * j + 1 - core, 2, False).wait_recv()
    for step in range(1, 8):
        block = lax.rem(exp + step, 8)
        remote(
            info, info_o.at[block], info_send.at[step - 1], info_recv.at[block], rep, block
        ).wait_recv()
    for copy in local:
        copy.wait()
    row_ways(exp, True, True, True, sent)
    for s in range(1, 4):
        pl.when(z >= s)(lambda s=s: row_ways(exp - 2 * s, False, True, False, sent))
        pl.when(z + s <= 3)(lambda s=s: row_ways(exp + 2 * s, False, False, True, sent))
    for k in range(3):
        for way in range(2):
            for h in range(2):
                w_own(k, h, way).wait_send()
            w_forward(k, way).wait_send()
    for step in range(1, 8):
        info_copy(step).wait_send()


def scatter_kernel(
    back, pg, pu, pd,
    back_o, rg, ru, rd,
    tmp, summed, back_send, back_recv, p_send, p_recv, local_sem,
):
    rep, exp = lax.axis_index("rep"), lax.axis_index("exp")
    x_rep, y_rep, diag = rep_neighbours(rep)
    greet(rep, exp, x_rep, y_rep, 8)
    terms, received = (pg, pu, pd), (rg, ru, rd)
    half = pg.shape[1] // 2
    part = (pl.ds(0, half), pl.ds(half, half))
    near = (x_rep, y_rep)

    def relay(k, way):
        return remote(
            terms[k].at[diag, part[way]], tmp.at[k, way],
            p_send.at[k, way, 0], p_recv.at[k, way, 0], near[way], exp,
        )

    def direct(k, way):
        return remote(
            terms[k].at[near[way], part[way]], received[k].at[way, part[way]],
            p_send.at[k, way, 1], p_recv.at[k, way, 1], near[way], exp,
        )

    def onward(k, way):
        return remote(
            summed.at[k, way], received[k].at[way, part[1 - way]],
            p_send.at[k, way, 2], p_recv.at[k, way, 2], near[way], exp,
        )

    def back_copy(step):
        other = lax.rem(exp + step, 8)
        return remote(
            back.at[other], back_o.at[exp], back_send.at[step - 1], back_recv.at[exp], rep, other
        )

    for k in range(3):
        for way in range(2):
            relay(k, way).start()
    for step in (4, 3, 5, 2, 6, 1, 7):
        back_copy(step).start()
    for k in range(3):
        for way in range(2):
            direct(k, way).start()
    own = pltpu.make_async_copy(back.at[exp], back_o.at[exp], local_sem)
    own.start()
    for k in range(3):
        for way in range(2):
            relay(k, way).wait_recv()
            rows = 64

            @pl.loop(0, half // rows)
            def _(i):
                at = pl.ds(pl.multiple_of(i * rows, rows), rows)
                mine = terms[k][
                    near[1 - way], pl.ds(pl.multiple_of(way * half + i * rows, rows), rows), :
                ]
                summed[k, 1 - way, at, :] = (
                    mine.astype(F32) + tmp[k, way, at, :].astype(F32)
                ).astype(BF16)

            onward(k, 1 - way).start()
    own.wait()
    for k in range(3):
        for way in range(2):
            direct(k, way).wait_recv()
            onward(k, way).wait_recv()
    for step in range(1, 8):
        block = lax.rem(exp + step, 8)
        remote(
            back.at[block], back_o.at[block], back_send.at[step - 1], back_recv.at[block], rep,
            block,
        ).wait_recv()
    for k in range(3):
        for way in range(2):
            relay(k, way).wait_send()
            direct(k, way).wait_send()
            onward(k, way).wait_send()
    for step in range(1, 8):
        back_copy(step).wait_send()


ANY = pl.BlockSpec(memory_space=pl.ANY)
VMEM = pl.BlockSpec(memory_space=pltpu.VMEM)
DMA = pltpu.SemaphoreType.DMA


def gather_all(tokens, grad_out, info, w_gate, w_up, w_down):
    rows = jax.ShapeDtypeStruct((8,) + tokens.shape, BF16)
    weights = jax.ShapeDtypeStruct((4,) + w_gate.shape, BF16)
    return pl.pallas_call(
        gather_kernel,
        out_shape=(rows, rows, jax.ShapeDtypeStruct((8,) + info.shape, F32)) + (weights,) * 3,
        in_specs=[ANY] * 6,
        out_specs=(ANY,) * 6,
        scratch_shapes=[
            DMA((2, 4, 3)), DMA((2, 8)), DMA((7,)), DMA((8,)),
            DMA((3, 2, 2)), DMA((3, 2)), DMA((3, 4, 2)), DMA((6,)),
        ],
        compiler_params=pltpu.CompilerParams(collective_id=0, has_side_effects=True),
    )(tokens, grad_out, info, w_gate, w_up, w_down)


def scatter_all(back, p_gate, p_up, p_down):
    _, depth, width = p_gate.shape
    got = jax.ShapeDtypeStruct((2, depth, width), BF16)
    return pl.pallas_call(
        scatter_kernel,
        out_shape=(jax.ShapeDtypeStruct(back.shape, BF16), got, got, got),
        in_specs=[ANY] + [VMEM] * 3,
        out_specs=(ANY,) * 4,
        scratch_shapes=[
            pltpu.VMEM((3, 2, depth // 2, width), BF16),
            pltpu.VMEM((3, 2, depth // 2, width), BF16),
            DMA((7,)), DMA((8,)), DMA((3, 2, 3)), DMA((3, 2, 3)), DMA,
        ],
        compiler_params=pltpu.CompilerParams(
            collective_id=1, has_side_effects=True, vmem_limit_bytes=32 * 1024 * 1024
        ),
    )(back, p_gate, p_up, p_down)


def expert_math(x_rows, g_rows, full_gate, full_up, full_down):
    pre_gate = jnp.dot(x_rows, full_gate, preferred_element_type=F32)
    pre_up = jnp.dot(x_rows, full_up, preferred_element_type=F32)
    hid_grad = jnp.dot(g_rows, full_down, preferred_element_type=F32)
    sig_gate = jax.nn.sigmoid(pre_gate)
    silu_gate = pre_gate * sig_gate
    hidden = (silu_gate * pre_up).astype(BF16)
    d_gate = (hid_grad * pre_up * sig_gate * (1.0 + pre_gate * (1.0 - sig_gate))).astype(BF16)
    d_up = (hid_grad * silu_gate).astype(BF16)
    row_grad = (against_cols(d_gate, full_gate) + against_cols(d_up, full_up)).astype(BF16)
    return hidden, d_gate, d_up, row_grad


def ranks_of(named):
    count = named.shape[-1]
    earlier = (jnp.arange(count)[:, None] < jnp.arange(count)[None, :]).astype(BF16)
    return jnp.dot(named.astype(BF16), earlier, preferred_element_type=F32).astype(jnp.int32)


def slots_of(routes, expert_count, slot_cap):
    tok_count = routes.shape[0]
    experts = jnp.arange(expert_count, dtype=jnp.int32)[:, None]
    named = (routes[:, 0][None, :] == experts) | (routes[:, 1][None, :] == experts)
    rank = jnp.where(named, ranks_of(named), slot_cap)
    held = rank[:, None, :] == jnp.arange(slot_cap, dtype=jnp.int32)[None, :, None]
    return held.reshape(expert_count * slot_cap, tok_count)


def block_of_mesh(tokens, grad_out, routes, gates, w_gate, w_up, w_down):
    tok_count, model_width = tokens.shape
    depth, width = w_gate.shape[1:]
    expert_count = lax.axis_size("exp")
    slot_cap = max(2, 2 * tok_count * routes.shape[1] // expert_count)
    rep, exp = lax.axis_index("rep"), lax.axis_index("exp")
    info = jnp.concatenate(
        [routes.T.astype(F32), gates.T, jnp.zeros((4, tok_count), F32)], axis=0
    )
    all_tok, all_grd, all_info, full_gate, full_up, full_down = gather_all(
        tokens, grad_out, info, w_gate[0], w_up[0], w_down[0]
    )
    full_gate, full_up, full_down = (
        w.reshape(4 * depth, width) for w in (full_gate, full_up, full_down)
    )
    mine = exp.astype(F32)
    first, second = all_info[:, 0, :] == mine, all_info[:, 1, :] == mine
    named = first | second
    gate = jnp.where(first, all_info[:, 2, :], jnp.where(second, all_info[:, 3, :], 0.0))
    rank = jnp.where(named, ranks_of(named), slot_cap)
    held = rank[:, None, :] == jnp.arange(slot_cap, dtype=jnp.int32)[None, :, None]
    pick = held.astype(BF16)
    slot_gate = jnp.sum(jnp.where(held, gate[:, None, :], 0.0), axis=2)
    into = functools.partial(
        lax.dot_general,
        dimension_numbers=(((2,), (1,)), ((0,), (0,))),
        preferred_element_type=F32,
    )
    x_rows = into(pick, all_tok).astype(BF16).reshape(expert_count * slot_cap, model_width)
    g_rows = (slot_gate[:, :, None] * into(pick, all_grd)).astype(BF16)
    g_rows = g_rows.reshape(expert_count * slot_cap, model_width)
    hidden, d_gate, d_up, row_grad = expert_math(x_rows, g_rows, full_gate, full_up, full_down)
    pairs = ((x_rows, d_gate), (x_rows, d_up), (g_rows, hidden))
    terms = [contract_rows(a, b).astype(BF16).reshape(4, depth, width) for a, b in pairs]
    returned, *received = scatter_all(
        row_grad.reshape(expert_count, slot_cap, model_width), *terms
    )
    grads = [
        contract_rows(lax.dynamic_slice_in_dim(a, rep * depth, depth, 1), b)
        + got[0].astype(F32) + got[1].astype(F32)
        for (a, b), got in zip(pairs, received)
    ]
    slots = slots_of(routes, expert_count, slot_cap).astype(BF16)
    grad_in = contract_rows(
        slots, returned.reshape(expert_count * slot_cap, model_width)
    ).astype(BF16)
    return (*(g[None] for g in grads), grad_in)


def any_mesh(tokens, grad_out, routes, gates, w_gate, w_up, w_down):
    tok_count, _ = tokens.shape
    expert_count = lax.axis_size("exp")
    slot_cap = max(2, 2 * tok_count * routes.shape[1] // expert_count)
    slots = slots_of(routes, expert_count, slot_cap)
    owner = jnp.repeat(jnp.arange(expert_count, dtype=jnp.int32), slot_cap)[:, None]
    pick = slots.astype(BF16)
    gate = jnp.where(routes[:, 0][None, :] == owner, gates[:, 0][None, :], gates[:, 1][None, :])
    slot_gate = jnp.sum(jnp.where(slots, gate, 0.0), axis=1)
    x_send = jnp.dot(pick, tokens, preferred_element_type=F32).astype(BF16)
    g_send = jnp.dot(pick, grad_out, preferred_element_type=F32)
    g_send = (slot_gate[:, None] * g_send).astype(BF16)
    x_rows = lax.all_to_all(x_send, "exp", split_axis=0, concat_axis=0, tiled=True)
    g_rows = lax.all_to_all(g_send, "exp", split_axis=0, concat_axis=0, tiled=True)
    full = [lax.all_gather(w[0], "rep", axis=0, tiled=True) for w in (w_gate, w_up, w_down)]
    hidden, d_gate, d_up, row_grad = expert_math(x_rows, g_rows, *full)
    returned = lax.all_to_all(row_grad, "exp", split_axis=0, concat_axis=0, tiled=True)
    grad_in = contract_rows(pick, returned).astype(BF16)
    grads = [
        lax.psum_scatter(contract_rows(a, b), "rep", scatter_dimension=0, tiled=True)[None]
        for a, b in ((x_rows, d_gate), (x_rows, d_up), (g_rows, hidden))
    ]
    return (*grads, grad_in)


def solution(mesh):
    rows = P(("rep", "exp"), None)
    weights = P("exp", "rep", None)
    kernels = mesh.shape["rep"] == 4 and mesh.shape["exp"] == 8
    return jax.shard_map(
        block_of_mesh if kernels else any_mesh,
        mesh=mesh,
        in_specs=(rows,) * 4 + (weights,) * 3,
        out_specs=(weights,) * 3 + (rows,),
        check_vma=False,
    )
```

```python
import functools

import jax
import jax.numpy as jnp
from jax import lax
from jax.experimental import pallas as pl
from jax.experimental.pallas import tpu as pltpu
from jax.sharding import PartitionSpec as P

MESH = pl.DeviceIdType.MESH
F32 = jnp.float32
BF16 = jnp.bfloat16


def contract_rows(left, right):
    return lax.dot_general(left, right, (((0,), (0,)), ((), ())), preferred_element_type=F32)


def against_cols(left, right):
    return lax.dot_general(left, right, (((1,), (1,)), ((), ())), preferred_element_type=F32)


def remote(src, dst, send_sem, recv_sem, rep, exp):
    return pltpu.make_async_remote_copy(
        src_ref=src,
        dst_ref=dst,
        send_sem=send_sem,
        recv_sem=recv_sem,
        device_id=(rep, exp),
        device_id_type=MESH,
    )


def greet(rep, exp, x_rep, y_rep, exp_count):
    barrier = pltpu.get_barrier_semaphore()
    for step in range(1, exp_count):
        other = lax.rem(exp + step, exp_count)
        pl.semaphore_signal(barrier, inc=1, device_id=(rep, other), device_id_type=MESH)
    for other in (x_rep, y_rep):
        pl.semaphore_signal(barrier, inc=1, device_id=(other, exp), device_id_type=MESH)
    pl.semaphore_wait(barrier, exp_count + 1)


def rep_neighbours(rep):
    return rep + 1 - 2 * lax.rem(rep, 2), lax.rem(rep + 2, 4), 3 - rep


def gather_kernel(
    tok, grd, info, wg, wu, wd,
    tok_o, grd_o, info_o, wg_o, wu_o, wd_o,
    row_send, row_recv, info_send, info_recv, w_send, w_fwd, w_recv, fetch_sem, local_sem,
    *staged,
):
    rep, exp = lax.axis_index("rep"), lax.axis_index("exp")
    x_rep, y_rep, diag = rep_neighbours(rep)
    z, core = lax.div(exp, 2), lax.rem(exp, 2)
    sibling = exp + 1 - 2 * core
    greet(rep, exp, x_rep, y_rep, 8)

    rows_in, rows_out = (tok, grd), (tok_o, grd_o)
    w_in, w_out = (wg, wu, wd), (wg_o, wu_o, wd_o)
    half = wg.shape[0] // 2
    part = (pl.ds(0, half), pl.ds(half, half))
    targets = (exp + 2, exp - 2, sibling)

    def row_copy(a, block, way, own):
        dst = rows_out[a].at[block]
        return remote(
            rows_in[a] if own else dst, dst,
            row_send.at[a, lax.div(block, 2), way], row_recv.at[a, block], rep, targets[way],
        )

    def row_ways(block, own, up, down, act):
        for a in range(2):
            if up:
                pl.when(z < 3)(lambda a=a: act(row_copy(a, block, 0, own)))
            if down:
                pl.when(z > 0)(lambda a=a: act(row_copy(a, block, 1, own)))
            act(row_copy(a, block, 2, own))

    def start(copy):
        copy.start()

    def sent(copy):
        copy.wait_send()

    def w_own(k, h, way):
        return remote(
            w_in[k].at[part[h]], w_out[k].at[rep, part[h]],
            w_send.at[k, h, way], w_recv.at[k, rep, h], (x_rep, y_rep)[way], exp,
        )

    def w_forward(k, way):
        block, h, to = ((x_rep, 0, y_rep), (y_rep, 1, x_rep))[way]
        ref = w_out[k].at[block, part[h]]
        return remote(ref, ref, w_fwd.at[k, way], w_recv.at[k, block, h], to, exp)

    def w_arrived(k, block, h):
        ref = w_out[k].at[block, part[h]]
        remote(ref, ref, w_fwd.at[k, 0], w_recv.at[k, block, h], y_rep, exp).wait_recv()

    def info_copy(step):
        other = lax.rem(exp + step, 8)
        return remote(
            info, info_o.at[exp], info_send.at[step - 1], info_recv.at[exp], rep, other
        )

    row_ways(exp, True, True, True, start)
    for h in range(2):
        for k in range(3):
            w_own(k, h, 0).start()
            w_own(k, 1 - h, 1).start()
    for step in range(1, 8):
        info_copy(step).start()
    kept = list(zip(
        (tok, grd, info, wg, wu, wd),
        staged,
        (tok_o.at[exp], grd_o.at[exp], info_o.at[exp], wg_o.at[rep], wu_o.at[rep], wd_o.at[rep]),
    ))
    fetch = [
        pltpu.make_async_copy(src, mid, fetch_sem.at[i]) for i, (src, mid, _) in enumerate(kept)
    ]
    local = [
        pltpu.make_async_copy(mid, dst, local_sem.at[i]) for i, (_, mid, dst) in enumerate(kept)
    ]
    for copy in fetch:
        copy.start()
    for first, second in zip(fetch, local):
        first.wait()
        second.start()

    for s in range(1, 4):
        @pl.when(z >= s)
        def _():
            block = exp - 2 * s
            for a in range(2):
                row_copy(a, block, 2, False).wait_recv()
            row_ways(block, False, True, False, start)

        @pl.when(z + s <= 3)
        def _():
            block = exp + 2 * s
            for a in range(2):
                row_copy(a, block, 2, False).wait_recv()
            row_ways(block, False, False, True, start)

        if s == 1:
            for k in range(3):
                w_arrived(k, x_rep, 0)
                w_forward(k, 0).start()
                w_arrived(k, y_rep, 1)
                w_forward(k, 1).start()

    for k in range(3):
        w_arrived(k, x_rep, 1)
        w_arrived(k, y_rep, 0)
        w_arrived(k, diag, 0)
        w_arrived(k, diag, 1)
    for j in range(4):
        for a in range(2):
            row_copy(a, 2 * j + 1 - core, 2, False).wait_recv()
    for step in range(1, 8):
        block = lax.rem(exp + step, 8)
        remote(
            info, info_o.at[block], info_send.at[step - 1], info_recv.at[block], rep, block
        ).wait_recv()
    for copy in local:
        copy.wait()
    row_ways(exp, True, True, True, sent)
    for s in range(1, 4):
        pl.when(z >= s)(lambda s=s: row_ways(exp - 2 * s, False, True, False, sent))
        pl.when(z + s <= 3)(lambda s=s: row_ways(exp + 2 * s, False, False, True, sent))
    for k in range(3):
        for way in range(2):
            for h in range(2):
                w_own(k, h, way).wait_send()
            w_forward(k, way).wait_send()
    for step in range(1, 8):
        info_copy(step).wait_send()


def scatter_kernel(
    back, pg, pu, pd,
    back_o, rg, ru, rd,
    tmp, summed, staged, back_send, back_recv, p_send, p_recv, fetch_sem, local_sem,
):
    rep, exp = lax.axis_index("rep"), lax.axis_index("exp")
    x_rep, y_rep, diag = rep_neighbours(rep)
    greet(rep, exp, x_rep, y_rep, 8)
    terms, received = (pg, pu, pd), (rg, ru, rd)
    half = pg.shape[1] // 2
    part = (pl.ds(0, half), pl.ds(half, half))
    near = (x_rep, y_rep)

    def relay(k, way):
        return remote(
            terms[k].at[diag, part[way]], tmp.at[k, way],
            p_send.at[k, way, 0], p_recv.at[k, way, 0], near[way], exp,
        )

    def direct(k, way):
        return remote(
            terms[k].at[near[way], part[way]], received[k].at[way, part[way]],
            p_send.at[k, way, 1], p_recv.at[k, way, 1], near[way], exp,
        )

    def onward(k, way):
        return remote(
            summed.at[k, way], received[k].at[way, part[1 - way]],
            p_send.at[k, way, 2], p_recv.at[k, way, 2], near[way], exp,
        )

    def back_copy(step):
        other = lax.rem(exp + step, 8)
        return remote(
            back.at[other], back_o.at[exp], back_send.at[step - 1], back_recv.at[exp], rep, other
        )

    for k in range(3):
        for way in range(2):
            relay(k, way).start()
    for step in (4, 3, 5, 2, 6, 1, 7):
        back_copy(step).start()
    for k in range(3):
        for way in range(2):
            direct(k, way).start()
    fetch = pltpu.make_async_copy(back.at[exp], staged, fetch_sem)
    fetch.start()
    fetch.wait()
    own = pltpu.make_async_copy(staged, back_o.at[exp], local_sem)
    own.start()
    for k in range(3):
        for way in range(2):
            relay(k, way).wait_recv()
            rows = 64

            @pl.loop(0, half // rows)
            def _(i):
                at = pl.ds(pl.multiple_of(i * rows, rows), rows)
                mine = terms[k][
                    near[1 - way], pl.ds(pl.multiple_of(way * half + i * rows, rows), rows), :
                ]
                summed[k, 1 - way, at, :] = (
                    mine.astype(F32) + tmp[k, way, at, :].astype(F32)
                ).astype(BF16)

            onward(k, 1 - way).start()
    own.wait()
    for k in range(3):
        for way in range(2):
            direct(k, way).wait_recv()
            onward(k, way).wait_recv()
    for step in range(1, 8):
        block = lax.rem(exp + step, 8)
        remote(
            back.at[block], back_o.at[block], back_send.at[step - 1], back_recv.at[block], rep,
            block,
        ).wait_recv()
    for k in range(3):
        for way in range(2):
            relay(k, way).wait_send()
            direct(k, way).wait_send()
            onward(k, way).wait_send()
    for step in range(1, 8):
        back_copy(step).wait_send()


ANY = pl.BlockSpec(memory_space=pl.ANY)
VMEM = pl.BlockSpec(memory_space=pltpu.VMEM)
DMA = pltpu.SemaphoreType.DMA


def gather_all(tokens, grad_out, info, w_gate, w_up, w_down):
    rows = jax.ShapeDtypeStruct((8,) + tokens.shape, BF16)
    weights = jax.ShapeDtypeStruct((4,) + w_gate.shape, BF16)
    return pl.pallas_call(
        gather_kernel,
        out_shape=(rows, rows, jax.ShapeDtypeStruct((8,) + info.shape, F32)) + (weights,) * 3,
        in_specs=[ANY] * 6,
        out_specs=(ANY,) * 6,
        scratch_shapes=[
            DMA((2, 4, 3)), DMA((2, 8)), DMA((7,)), DMA((8,)),
            DMA((3, 2, 2)), DMA((3, 2)), DMA((3, 4, 2)), DMA((6,)), DMA((6,)),
        ]
        + [
            pltpu.VMEM(a.shape, a.dtype)
            for a in (tokens, grad_out, info, w_gate, w_up, w_down)
        ],
        compiler_params=pltpu.CompilerParams(
            collective_id=0, has_side_effects=True, vmem_limit_bytes=16 * 1024 * 1024
        ),
    )(tokens, grad_out, info, w_gate, w_up, w_down)


def scatter_all(back, p_gate, p_up, p_down):
    _, depth, width = p_gate.shape
    got = jax.ShapeDtypeStruct((2, depth, width), BF16)
    return pl.pallas_call(
        scatter_kernel,
        out_shape=(jax.ShapeDtypeStruct(back.shape, BF16), got, got, got),
        in_specs=[ANY] + [VMEM] * 3,
        out_specs=(ANY,) * 4,
        scratch_shapes=[
            pltpu.VMEM((3, 2, depth // 2, width), BF16),
            pltpu.VMEM((3, 2, depth // 2, width), BF16),
            pltpu.VMEM(back.shape[1:], BF16),
            DMA((7,)), DMA((8,)), DMA((3, 2, 3)), DMA((3, 2, 3)), DMA, DMA,
        ],
        compiler_params=pltpu.CompilerParams(
            collective_id=1, has_side_effects=True, vmem_limit_bytes=32 * 1024 * 1024
        ),
    )(back, p_gate, p_up, p_down)


def expert_math(x_rows, g_rows, full_gate, full_up, full_down):
    pre_gate = jnp.dot(x_rows, full_gate, preferred_element_type=F32)
    pre_up = jnp.dot(x_rows, full_up, preferred_element_type=F32)
    hid_grad = jnp.dot(g_rows, full_down, preferred_element_type=F32)
    sig_gate = jax.nn.sigmoid(pre_gate)
    silu_gate = pre_gate * sig_gate
    hidden = (silu_gate * pre_up).astype(BF16)
    d_gate = (hid_grad * pre_up * sig_gate * (1.0 + pre_gate * (1.0 - sig_gate))).astype(BF16)
    d_up = (hid_grad * silu_gate).astype(BF16)
    row_grad = (against_cols(d_gate, full_gate) + against_cols(d_up, full_up)).astype(BF16)
    return hidden, d_gate, d_up, row_grad


def ranks_of(named):
    count = named.shape[-1]
    earlier = (jnp.arange(count)[:, None] < jnp.arange(count)[None, :]).astype(BF16)
    return jnp.dot(named.astype(BF16), earlier, preferred_element_type=F32).astype(jnp.int32)


def slots_of(routes, expert_count, slot_cap):
    tok_count = routes.shape[0]
    experts = jnp.arange(expert_count, dtype=jnp.int32)[:, None]
    named = (routes[:, 0][None, :] == experts) | (routes[:, 1][None, :] == experts)
    rank = jnp.where(named, ranks_of(named), slot_cap)
    held = rank[:, None, :] == jnp.arange(slot_cap, dtype=jnp.int32)[None, :, None]
    return held.reshape(expert_count * slot_cap, tok_count)


def block_of_mesh(tokens, grad_out, routes, gates, w_gate, w_up, w_down):
    tok_count, model_width = tokens.shape
    depth, width = w_gate.shape[1:]
    expert_count = lax.axis_size("exp")
    slot_cap = max(2, 2 * tok_count * routes.shape[1] // expert_count)
    rep, exp = lax.axis_index("rep"), lax.axis_index("exp")
    info = jnp.concatenate(
        [routes.T.astype(F32), gates.T, jnp.zeros((4, tok_count), F32)], axis=0
    )
    all_tok, all_grd, all_info, full_gate, full_up, full_down = gather_all(
        tokens, grad_out, info, w_gate[0], w_up[0], w_down[0]
    )
    full_gate, full_up, full_down = (
        w.reshape(4 * depth, width) for w in (full_gate, full_up, full_down)
    )
    mine = exp.astype(F32)
    first, second = all_info[:, 0, :] == mine, all_info[:, 1, :] == mine
    named = first | second
    gate = jnp.where(first, all_info[:, 2, :], jnp.where(second, all_info[:, 3, :], 0.0))
    rank = jnp.where(named, ranks_of(named), slot_cap)
    held = rank[:, None, :] == jnp.arange(slot_cap, dtype=jnp.int32)[None, :, None]
    pick = held.astype(BF16)
    slot_gate = jnp.sum(jnp.where(held, gate[:, None, :], 0.0), axis=2)
    into = functools.partial(
        lax.dot_general,
        dimension_numbers=(((2,), (1,)), ((0,), (0,))),
        preferred_element_type=F32,
    )
    x_rows = into(pick, all_tok).astype(BF16).reshape(expert_count * slot_cap, model_width)
    g_rows = (slot_gate[:, :, None] * into(pick, all_grd)).astype(BF16)
    g_rows = g_rows.reshape(expert_count * slot_cap, model_width)
    hidden, d_gate, d_up, row_grad = expert_math(x_rows, g_rows, full_gate, full_up, full_down)
    pairs = ((x_rows, d_gate), (x_rows, d_up), (g_rows, hidden))
    terms = [contract_rows(a, b).astype(BF16).reshape(4, depth, width) for a, b in pairs]
    returned, *received = scatter_all(
        row_grad.reshape(expert_count, slot_cap, model_width), *terms
    )
    grads = [
        lax.dynamic_index_in_dim(term, rep, 0, keepdims=False).astype(F32)
        + got[0].astype(F32) + got[1].astype(F32)
        for term, got in zip(terms, received)
    ]
    slots = slots_of(routes, expert_count, slot_cap).astype(BF16)
    grad_in = contract_rows(
        slots, returned.reshape(expert_count * slot_cap, model_width)
    ).astype(BF16)
    return (*(g[None] for g in grads), grad_in)


def any_mesh(tokens, grad_out, routes, gates, w_gate, w_up, w_down):
    tok_count, _ = tokens.shape
    expert_count = lax.axis_size("exp")
    slot_cap = max(2, 2 * tok_count * routes.shape[1] // expert_count)
    slots = slots_of(routes, expert_count, slot_cap)
    owner = jnp.repeat(jnp.arange(expert_count, dtype=jnp.int32), slot_cap)[:, None]
    pick = slots.astype(BF16)
    gate = jnp.where(routes[:, 0][None, :] == owner, gates[:, 0][None, :], gates[:, 1][None, :])
    slot_gate = jnp.sum(jnp.where(slots, gate, 0.0), axis=1)
    x_send = jnp.dot(pick, tokens, preferred_element_type=F32).astype(BF16)
    g_send = jnp.dot(pick, grad_out, preferred_element_type=F32)
    g_send = (slot_gate[:, None] * g_send).astype(BF16)
    x_rows = lax.all_to_all(x_send, "exp", split_axis=0, concat_axis=0, tiled=True)
    g_rows = lax.all_to_all(g_send, "exp", split_axis=0, concat_axis=0, tiled=True)
    full = [lax.all_gather(w[0], "rep", axis=0, tiled=True) for w in (w_gate, w_up, w_down)]
    hidden, d_gate, d_up, row_grad = expert_math(x_rows, g_rows, *full)
    returned = lax.all_to_all(row_grad, "exp", split_axis=0, concat_axis=0, tiled=True)
    grad_in = contract_rows(pick, returned).astype(BF16)
    grads = [
        lax.psum_scatter(contract_rows(a, b), "rep", scatter_dimension=0, tiled=True)[None]
        for a, b in ((x_rows, d_gate), (x_rows, d_up), (g_rows, hidden))
    ]
    return (*grads, grad_in)


def solution(mesh):
    rows = P(("rep", "exp"), None)
    weights = P("exp", "rep", None)
    kernels = mesh.shape["rep"] == 4 and mesh.shape["exp"] == 8
    return jax.shard_map(
        block_of_mesh if kernels else any_mesh,
        mesh=mesh,
        in_specs=(rows,) * 4 + (weights,) * 3,
        out_specs=(weights,) * 3 + (rows,),
        check_vma=False,
    )
```
